512 devices in a mesh: island: 16 (over y, core), fsdp: 32 (over z, x).
Axes of the slice: x: 4, y: 8, z: 8, core: 2. Of those that a mesh axis runs over, the one named last changes fastest.
Arguments:
- delta: bfloat16 [16, 2048, 4096], P('island', 'fsdp'), may hold values from -6 to 6
- error: float32 [16, 2048, 4096], P('island', 'fsdp'), may hold values from -6 to 6
- param: bfloat16 [2048, 4096], P('fsdp'), may hold values from -6 to 6
- velocity: bfloat16 [2048, 4096], P('fsdp'), may hold values from -4 to 4
- piece_ids: int32 [32, 32, 16], P('fsdp'), may hold values from 0 to 2047, as said below
- piece_counts: int32 [32, 32], P('fsdp'), may hold values from 8 to 16, as said below
Outputs:
- new_error: float32 [16, 2048, 4096], P('island', 'fsdp')
- new_param: bfloat16 [2048, 4096], P('fsdp')
- new_velocity: bfloat16 [2048, 4096], P('fsdp')
- compressed: float32 [32, 32, 16, 128], P('fsdp')
The draws below stay inside these ranges and needn't reach their ends.
Inputs may be any that keep to these rules, and one draw needn't show every extreme that they name: `piece_ids`: within one shard's lists all entries are distinct, entries past the count included; those are ignored. `piece_counts`: one owner receives exactly 16 live entries from every shard.
All inputs are finite; a program needn't handle non-finite values.
Results may differ from the reference program's by a relative error of at most 0.001.
Values sent between devices are 32-bit elements; how exact they have to be, the bound alone decides.
A program may use at most 64 MiB of HBM per device.

```python
import jax
import jax.numpy as jnp
from jax import lax

BS = 64
COLS = 4096
CAP = 16
ROWS = 2048
NPIECE = 2048
ISLANDS = 16
N_FSDP = 32


def draw_piece_ids(key, part):
    key = jax.random.fold_in(key, 11)
    keys = jax.random.split(key, N_FSDP)

    def one_shard(shard_key):
        return jax.random.permutation(shard_key, NPIECE)[:N_FSDP * CAP]
    lists = jax.vmap(one_shard)(keys)
    return lists.reshape(N_FSDP, N_FSDP, CAP).astype(jnp.int32)


def draw_piece_counts(key, part):
    key = jax.random.fold_in(key, 23)
    base_key, hot_key = jax.random.split(key)
    base = jax.random.randint(base_key, (N_FSDP, N_FSDP), CAP // 2, CAP + 1)
    hottest = jax.random.randint(hot_key, (), 0, N_FSDP)
    owners = jnp.arange(N_FSDP, dtype=jnp.int32)[None, :]
    return jnp.where(owners == hottest, CAP, base).astype(jnp.int32)


def level_of(own_key, dims, cuts, smallest, high):
    def one(dim, blocks):
        steps = jax.random.uniform(jax.random.fold_in(jax.random.fold_in(own_key, 6), dim), (blocks,), jnp.float32, smallest / len(cuts), high / len(cuts))
        return jnp.repeat(jnp.exp(steps), dims[dim] // blocks).reshape((-1,) + (1,) * (len(dims) - dim - 1))

    loudness = one(*cuts[0])
    for cut in cuts[1:]:
        loudness = loudness * one(*cut)
    return loudness


def normal_values(key, dims, deviation, limit, shards=(), kind=jnp.bfloat16):
    gain = level_of(key, dims, shards, -0.22, 0.18) if shards else 1.0
    entries = jax.random.normal(key, dims, jnp.float32) * deviation * gain
    return jnp.minimum(jnp.maximum(entries, -limit), limit).astype(kind)


def setup_inputs(seed: int = 0) -> dict:
    streams_of = jax.random.split(jax.random.key(seed), 7)
    return {
        "delta": normal_values(streams_of[0], (ISLANDS, ROWS, COLS), 1.0, 6.0, ((0, 16), (1, 32))),
        "error": normal_values(streams_of[1], (ISLANDS, ROWS, COLS), 1.0, 6.0, ((0, 16), (1, 32)), jnp.float32),
        "param": normal_values(streams_of[2], (ROWS, COLS), 1.0, 6.0, ((0, 32),)),
        "velocity": normal_values(streams_of[3], (ROWS, COLS), 0.3, 4.0, ((0, 32),)),
        "piece_ids": draw_piece_ids(jax.random.fold_in(streams_of[6], 71), 0),
        "piece_counts": draw_piece_counts(jax.random.fold_in(streams_of[6], 71), 0),
    }


decay_rate = 0.9
outer_rate = 0.7
nesterov = 0.9
eps_value = 1e-06

def cosine_table():
    freq = jnp.arange(BS, dtype=jnp.int32)[:, None].astype(jnp.float32)
    place = jnp.arange(BS, dtype=jnp.int32)[None, :].astype(jnp.float32)
    scale = jnp.where(freq == 0.0, jnp.sqrt(1.0 / BS), jnp.sqrt(2.0 / BS))
    return (scale * jnp.cos(jnp.pi * (2.0 * place + 1.0) * freq / (2.0 * BS))).astype(jnp.float32)

def transform(field, table, column_table):
    rows = field.shape[0]
    right = jnp.dot(field.reshape(-1, 128), column_table, precision=lax.Precision.HIGHEST)
    right = right.reshape(rows // BS, BS, COLS // 128, 128)
    left = jnp.einsum('kn,rnqj->rqkj', table, right, precision=lax.Precision.HIGHEST)
    return left.reshape(-1, 128)

def inverse(pieces, table, column_table):
    rows = pieces.shape[0] * 128 // COLS
    blocks = pieces.reshape(rows // BS, COLS // 128, BS, 128)
    left = jnp.einsum('kn,rqkj->rnqj', table, blocks, precision=lax.Precision.HIGHEST)
    back = jnp.dot(left.reshape(-1, 128), column_table.T, precision=lax.Precision.HIGHEST)
    return back.reshape(rows, COLS)

def reference(delta, error, param, velocity, piece_ids, piece_counts):
    table = cosine_table()
    column_table = jnp.kron(jnp.eye(2, dtype=jnp.float32), table.T)
    offsets = (jnp.arange(N_FSDP, dtype=jnp.int32) * NPIECE).astype(jnp.int32)
    global_ids = (piece_ids + offsets[:, None, None]).astype(jnp.int32)
    slots = jnp.arange(CAP, dtype=jnp.int32)[None, None, :]
    active = (slots < piece_counts[:, :, None]).astype(jnp.float32)
    flat_ids = global_ids.reshape(-1)
    kept_mask = jnp.zeros((N_FSDP * NPIECE,), jnp.float32).at[flat_ids].set(active.reshape(-1))

    def per_island(summed, inputs):
        grad, feedback = inputs
        momentum = decay_rate * feedback + grad.astype(jnp.float32)
        coefficients = transform(momentum, table, column_table)
        chosen = coefficients[global_ids] * active[..., None]
        renewed = momentum - inverse(coefficients * kept_mask[:, None], table, column_table)
        return (summed + chosen, renewed)
    start = jnp.zeros((N_FSDP, N_FSDP, CAP, 128), jnp.float32)
    total, new_error = lax.scan(per_island, start, (delta, error))
    normed = total / jnp.sqrt(lax.optimization_barrier(jnp.mean(total * total, axis=-1, keepdims=True)) + eps_value)
    compressed = jnp.transpose(normed, (1, 0, 2, 3))
    scattered = jnp.zeros((N_FSDP * NPIECE, 128), jnp.float32).at[flat_ids].add(normed.reshape(-1, 128))
    update = inverse(scattered, table, column_table)
    moved = nesterov * velocity.astype(jnp.float32) + update
    new_velocity = moved.astype(jnp.bfloat16)
    new_param = (param.astype(jnp.float32) - outer_rate * (update + nesterov * moved)).astype(jnp.bfloat16)
    return (new_error, new_param, new_velocity, compressed)
```

```python
import functools
import math

import jax
import jax.numpy as jnp
import ml_dtypes
import numpy as np
from jax import lax
from jax.experimental import pallas as pl
from jax.experimental.pallas import tpu as pltpu
from jax.sharding import PartitionSpec as P

MESH = pl.DeviceIdType.MESH
F32 = jnp.float32
BF16 = jnp.bfloat16

decay_rate = 0.9
outer_rate = 0.7
nesterov = 0.9
eps_value = 1e-06

SIDE = 64
WIDE = 128
FAR_FIRST = (4, 3, 5, 2, 6, 1, 7)


def cosine_table(side):
    freq = np.arange(side, dtype=np.float64)[:, None]
    place = np.arange(side, dtype=np.float64)[None, :]
    scale = np.where(freq == 0, math.sqrt(1.0 / side), math.sqrt(2.0 / side))
    return scale * np.cos(math.pi * (2.0 * place + 1.0) * freq / (2.0 * side))


def halves(table):
    high = table.astype(np.float32).astype(ml_dtypes.bfloat16)
    low = (table - high.astype(np.float64)).astype(ml_dtypes.bfloat16)
    return high, low


def split(values):
    high = values.astype(BF16)
    low = (values - high.astype(F32)).astype(BF16)
    return high, low


def iota(shape, dim):
    return lax.broadcasted_iota(jnp.int32, shape, dim)


def kernel(
    delta, error, param, velocity, ids, counts, rows_fwd, rows_inv, cols_fwd,
    new_error, new_param, new_velocity, compressed,
    ids_s, counts_s, ids_v, counts_v, fwd, inv, cols, d_v, x_v, p_v, v_v, y_v, stack, hot, mask_v, ne_v,
    t_sib, t_own, t_got, part, got, ret, sent, held,
    in_sem, out_sem, sib_sem, rs_send, rs_recv, ag_send, ag_recv, rel_sem, b_send, b_own, b_recv, fin_sem,
    ready_x, ready_y,
):
    i = lax.axis_index("island")
    f = lax.axis_index("fsdp")
    y = lax.div(i, 2)
    core = lax.rem(i, 2)
    z = lax.div(f, 4)
    x = lax.rem(f, 4)
    sibling = (2 * y + (1 - core), f)
    width = error.shape[2]
    step = width // 4
    blocks = step // WIDE

    def y_peer(d):
        return (2 * lax.rem(y + d, 8) + core, f)

    barrier = pltpu.get_barrier_semaphore()
    near = [sibling]
    near += [y_peer(d) for d in range(1, 8)]
    near += [(i, 4 * lax.rem(z + d, 8) + x) for d in range(1, 8)]
    x_line = [(i, 4 * z + lax.rem(x + d, 4)) for d in range(1, 4)]
    near += x_line
    for other in near:
        pl.semaphore_signal(barrier, inc=1, device_id=other, device_id_type=MESH)

    loads = {}

    def load(name, src, dst):
        copy = pltpu.make_async_copy(src, dst, in_sem.at[len(loads)])
        copy.start()
        loads[name] = copy

    load("ids_s", ids.at[0], ids_s)
    load("fwd", rows_fwd, fwd)
    for c in range(4):
        at = pl.ds(c * step, step)
        load(f"e{c}", error.at[0, :, at], x_v.at[:, at])
        load(f"d{c}", delta.at[0, :, at], d_v.at[:, at])
    load("ids_v", ids.at[0], ids_v)
    load("counts_v", counts, counts_v)
    load("counts_s", counts, counts_s)
    load("inv", rows_inv, inv)
    load("cols", cols_fwd, cols)
    load("param", param, p_v)
    load("velocity", velocity, v_v)

    loads["fwd"].wait()
    for c in range(4):
        at = pl.ds(c * step, step)
        loads[f"e{c}"].wait()
        loads[f"d{c}"].wait()
        momentum = decay_rate * x_v[:, at] + d_v[:, at].astype(F32)
        x_v[:, at] = momentum
        high, low = split(momentum)
        stack[0:64, :] = high
        stack[64:128, :] = low
        stack[128:192, :] = high
        field = jnp.dot(fwd[...], stack[...], preferred_element_type=F32)
        for j in range(blocks):
            y_v[pl.ds((c * blocks + j) * SIDE, SIDE), :] = field[:, j * WIDE:(j + 1) * WIDE]

    loads["ids_s"].wait()

    def gather(side, out):
        @pl.loop(0, 32, unroll=4)
        def _(o):
            for k in range(8):
                out[pl.ds(o * 8 + k, 1), :] = y_v[pl.ds(ids_s[o, 8 * side + k], 1), :]

    gather(1 - core, t_sib)
    pl.semaphore_wait(barrier, len(near))
    for other in x_line:
        pl.semaphore_signal(ready_x, inc=1, device_id=other, device_id_type=MESH)
    to_sib = pltpu.make_async_remote_copy(
        src_ref=t_sib, dst_ref=t_got, send_sem=sib_sem.at[0], recv_sem=sib_sem.at[1],
        device_id=sibling, device_id_type=MESH)
    to_sib.start()
    gather(core, t_own)
    to_sib.wait_recv()

    rs = []
    for d in FAR_FIRST + (0,):
        there = lax.rem(y + d, 8)
        at = pl.ds(pl.multiple_of(there * 32, 32), 32)
        part[at, :] = t_own[at, :] + t_got[at, :]
        if d:
            copy = pltpu.make_async_remote_copy(
                src_ref=part.at[at], dst_ref=got.at[d], send_sem=rs_send.at[d], recv_sem=rs_recv.at[d],
                device_id=y_peer(d), device_id_type=MESH)
            copy.start()
            rs.append(copy)

    loads["ids_v"].wait()
    loads["counts_v"].wait()
    loads["inv"].wait()
    eye = iota((32, 32), 0) == iota((32, 32), 1)
    count_column = jnp.sum(jnp.where(eye, counts_v[...].astype(F32), 0.0), axis=1, keepdims=True)
    slot = iota((32, 16), 1).astype(F32)
    listed = jnp.where(slot < count_column, ids_v[...].astype(F32), -1.0)
    entry = iota((16, 512), 1)
    pick = jnp.where(iota((16, 512), 0) == 8 * (entry // 256) + entry % 8, 1.0, 0.0).astype(F32)
    spread = jnp.dot(listed, pick, precision=lax.Precision.HIGHEST, preferred_element_type=F32)
    entry = iota((32, 512), 1)
    spread = jnp.where(iota((32, 512), 0) == (entry // 8) % 32, spread, 0.0)
    place = jnp.sum(spread, axis=0, keepdims=True).astype(jnp.int32)
    row_hot = jnp.where(iota((64, 512), 0) == (place & 63), 1.0, 0.0).astype(BF16)
    block_hot = jnp.where(iota((32, 512), 0) == (place >> 6), 1.0, 0.0).astype(BF16)
    mask_v[...] = lax.dot_general(row_hot, block_hot, (((1,), (1,)), ((), ())), preferred_element_type=F32)

    out_copies = []

    def put(src, dst):
        copy = pltpu.make_async_copy(src, dst, out_sem.at[len(out_copies)])
        copy.start()
        out_copies.append(copy)

    def stack_block(j, values):
        at = pl.ds(j * WIDE, WIDE)
        high, low = split(values)
        stack[0:64, at] = high
        stack[64:128, at] = low
        stack[128:192, at] = high

    def error_part(c):
        at = pl.ds(c * step, step)
        for j in range(blocks):
            q = c * blocks + j
            stack_block(j, y_v[pl.ds(q * SIDE, SIDE), :] * mask_v[:, q:q + 1])
        kept = jnp.dot(inv[...], stack[...], preferred_element_type=F32)
        ne_v[:, at] = x_v[:, at] - kept
        put(ne_v.at[:, at], new_error.at[0, :, at])

    error_part(0)
    error_part(1)
    pl.semaphore_wait(ready_x, 3)
    for d in range(1, 8):
        pl.semaphore_signal(ready_y, inc=1, device_id=y_peer(d), device_id_type=MESH)
    error_part(2)
    error_part(3)

    @pl.loop(0, 32)
    def _(q):
        at = pl.ds(pl.multiple_of(q * SIDE, SIDE), SIDE)
        hot[at, :] = jnp.where(iota((SIDE, 512), 0) + q * SIDE == place, 1.0, 0.0).astype(BF16)

    loads["counts_s"].wait()
    loads["cols"].wait()
    for copy in rs:
        copy.wait_recv()
    mine = pl.ds(pl.multiple_of(y * 32, 32), 32)
    total = part[mine, :]
    for d in range(1, 8):
        total = total + got[d]
    alive = []
    for r in range(4):
        live = iota((8, WIDE), 0) + 8 * core < counts_s[0, 4 * y + r]
        alive.append(jnp.where(live, total[8 * r:8 * r + 8], 0.0))
    total = jnp.concatenate(alive, axis=0)
    normed = total / jnp.sqrt(jnp.mean(total * total, axis=1, keepdims=True) + eps_value)
    ret[core, mine, :] = normed
    ag = []
    for d in FAR_FIRST:
        copy = pltpu.make_async_remote_copy(
            src_ref=ret.at[core, mine], dst_ref=ret.at[core, mine], send_sem=ag_send.at[d], recv_sem=ag_recv.at[d],
            device_id=y_peer(d), device_id_type=MESH)
        copy.start()
        ag.append(copy)
    high, low = split(normed)
    sent[...] = (
        jnp.dot(high, cols[0], preferred_element_type=F32)
        + jnp.dot(low, cols[0], preferred_element_type=F32)
        + jnp.dot(high, cols[1], preferred_element_type=F32)
    )
    pl.semaphore_wait(ready_y, 7)
    owner_sends = []
    for d in FAR_FIRST:
        for r in range(4):
            copy = pltpu.make_async_remote_copy(
                src_ref=sent.at[pl.ds(8 * r, 8)], dst_ref=held.at[f], send_sem=b_send.at[0], recv_sem=b_recv.at[0],
                device_id=(2 * lax.rem(y + d, 8) + core, 4 * y + r), device_id_type=MESH)
            copy.start()
    for r in range(4):
        here = 4 * y + r == f

        @pl.when(here)
        def _():
            pltpu.make_async_copy(sent.at[pl.ds(8 * r, 8)], held.at[f], b_recv.at[0]).start()

        @pl.when(jnp.logical_not(here))
        def _():
            pltpu.make_async_remote_copy(
                src_ref=sent.at[pl.ds(8 * r, 8)], dst_ref=held.at[f], send_sem=b_own.at[r], recv_sem=b_recv.at[0],
                device_id=(i, 4 * y + r), device_id_type=MESH).start()

    for copy in ag:
        copy.wait_recv()
    relay = pltpu.make_async_remote_copy(
        src_ref=ret.at[core], dst_ref=ret.at[core], send_sem=rel_sem.at[0], recv_sem=rel_sem.at[1],
        device_id=sibling, device_id_type=MESH)
    relay.start()
    loads["param"].wait()
    loads["velocity"].wait()
    relay.wait_recv()
    high, low = split(jnp.concatenate([ret[0], ret[1]], axis=0))
    both = jnp.concatenate([high, low], axis=1)
    for c in range(4):
        at = pl.ds(c * step, step)
        pieces = jnp.dot(hot[pl.ds(c * blocks * SIDE, blocks * SIDE), :], both, preferred_element_type=F32)
        for j in range(blocks):
            block = pieces[j * SIDE:(j + 1) * SIDE]
            stack_block(j, block[:, :WIDE] + block[:, WIDE:])
        update = jnp.dot(inv[...], stack[...], preferred_element_type=F32)
        moved = nesterov * v_v[:, at].astype(F32) + update
        p_v[:, at] = (p_v[:, at].astype(F32) - outer_rate * (update + nesterov * moved)).astype(BF16)
        v_v[:, at] = moved.astype(BF16)
        put(v_v.at[:, at], new_velocity.at[:, at])
        put(p_v.at[:, at], new_param.at[:, at])

    pltpu.make_async_copy(held, held, b_recv.at[0]).wait()
    half = compressed.at[0, :, pl.ds(pl.multiple_of(8 * core, 8), 8), :]
    finish = pltpu.make_async_remote_copy(
        src_ref=held, dst_ref=half, send_sem=fin_sem.at[0], recv_sem=fin_sem.at[1],
        device_id=sibling, device_id_type=MESH)
    finish.start()
    put(held, half)
    finish.wait_recv()

    for copy in out_copies:
        copy.wait()
    to_sib.wait_send()
    for copy in rs + ag + [relay, finish]:
        copy.wait_send()
    out_rows = pl.ds(0, 28 * 8)
    pltpu.make_async_copy(part.at[out_rows], part.at[out_rows], b_send.at[0]).wait()
    for r in range(4):
        @pl.when(4 * y + r != f)
        def _():
            pltpu.make_async_remote_copy(
                src_ref=sent.at[pl.ds(8 * r, 8)], dst_ref=held.at[f], send_sem=b_own.at[r], recv_sem=b_recv.at[0],
                device_id=(i, 4 * y + r), device_id_type=MESH).wait_send()


def shards(delta, error, param, velocity, piece_ids, piece_counts):
    table = cosine_table(SIDE)
    high, low = halves(table)
    rows_fwd = jnp.asarray(np.concatenate([high, high, low], axis=1))
    rows_inv = jnp.asarray(np.concatenate([high.T, high.T, low.T], axis=1))
    cols_fwd = jnp.asarray(np.stack(halves(np.kron(np.eye(2), table.T))))
    rows, width = param.shape
    any_space = pl.BlockSpec(memory_space=pl.ANY)
    dma = pltpu.SemaphoreType.DMA
    step = width // 4
    return pl.pallas_call(
        kernel,
        out_shape=(
            jax.ShapeDtypeStruct(error.shape, F32),
            jax.ShapeDtypeStruct(param.shape, BF16),
            jax.ShapeDtypeStruct(param.shape, BF16),
            jax.ShapeDtypeStruct((1, 32, 16, WIDE), F32),
        ),
        in_specs=[any_space] * 9,
        out_specs=(any_space,) * 4,
        scratch_shapes=[
            pltpu.SMEM((32, 16), jnp.int32),
            pltpu.SMEM((1, 32), jnp.int32),
            pltpu.VMEM((32, 16), jnp.int32),
            pltpu.VMEM((1, 32), jnp.int32),
            pltpu.VMEM((64, 192), BF16),
            pltpu.VMEM((64, 192), BF16),
            pltpu.VMEM((2, 128, 128), BF16),
            pltpu.VMEM((rows, width), BF16),
            pltpu.VMEM((rows, width), F32),
            pltpu.VMEM((rows, width), BF16),
            pltpu.VMEM((rows, width), BF16),
            pltpu.VMEM((2048, WIDE), F32),
            pltpu.VMEM((192, step), BF16),
            pltpu.VMEM((2048, 512), BF16),
            pltpu.VMEM((64, 32), F32),
            pltpu.VMEM((rows, width), F32),
            pltpu.VMEM((256, WIDE), F32),
            pltpu.VMEM((256, WIDE), F32),
            pltpu.VMEM((256, WIDE), F32),
            pltpu.VMEM((256, WIDE), F32),
            pltpu.VMEM((8, 32, WIDE), F32),
            pltpu.VMEM((2, 256, WIDE), F32),
            pltpu.VMEM((32, WIDE), F32),
            pltpu.VMEM((32, 8, WIDE), F32),
            dma((20,)),
            dma((16,)),
            dma((2,)),
            dma((8,)),
            dma((8,)),
            dma((8,)),
            dma((8,)),
            dma((2,)),
            dma((1,)),
            dma((4,)),
            dma((1,)),
            dma((2,)),
            pltpu.SemaphoreType.REGULAR,
            pltpu.SemaphoreType.REGULAR,
        ],
        compiler_params=pltpu.CompilerParams(
            collective_id=0, has_side_effects=True, vmem_limit_bytes=56 << 20),
        name="sync",
    )(delta, error, param, velocity, piece_ids, piece_counts, rows_fwd, rows_inv, cols_fwd)


def solution(mesh):
    in_specs = (
        P("island", "fsdp", None),
        P("island", "fsdp", None),
        P("fsdp", None),
        P("fsdp", None),
        P("fsdp", None, None),
        P("fsdp", None),
    )
    out_specs = (
        P("island", "fsdp", None),
        P("fsdp", None),
        P("fsdp", None),
        P("fsdp", None, None, None),
    )
    return jax.shard_map(shards, mesh=mesh, in_specs=in_specs, out_specs=out_specs, check_vma=False)
```

```python
import functools
import math

import jax
import jax.numpy as jnp
import ml_dtypes
import numpy as np
from jax import lax
from jax.experimental import pallas as pl
from jax.experimental.pallas import tpu as pltpu
from jax.sharding import PartitionSpec as P

MESH = pl.DeviceIdType.MESH
F32 = jnp.float32
BF16 = jnp.bfloat16

decay_rate = 0.9
outer_rate = 0.7
nesterov = 0.9
eps_value = 1e-06

SIDE = 64
WIDE = 128
PEERS = 7


def far(n):
    return 4 + (1 - 2 * lax.rem(n, 2)) * lax.div(n + 1, 2)


def cosine_table(side):
    freq = np.arange(side, dtype=np.float64)[:, None]
    place = np.arange(side, dtype=np.float64)[None, :]
    scale = np.where(freq == 0, math.sqrt(1.0 / side), math.sqrt(2.0 / side))
    return scale * np.cos(math.pi * (2.0 * place + 1.0) * freq / (2.0 * side))


def halves(table):
    high = table.astype(np.float32).astype(ml_dtypes.bfloat16)
    low = (table - high.astype(np.float64)).astype(ml_dtypes.bfloat16)
    return high, low


def split(values):
    high = values.astype(BF16)
    low = (values - high.astype(F32)).astype(BF16)
    return high, low


def iota(shape, dim):
    return lax.broadcasted_iota(jnp.int32, shape, dim)


def kernel(
    delta, error, param, velocity, ids, counts, rows_fwd, rows_inv, cols_fwd,
    new_error, new_param, new_velocity, compressed,
    ids_s, counts_s, ids_v, counts_v, fwd, inv, cols, d_v, x_v, p_v, v_v, y_v, stack, hot, mask_v,
    t_sib, t_own, t_got, part, got, ret, sent,
    in_sem, field_sem, sib_sem, rs_send, rs_recv, ag_send, ag_recv, rel_sem, b_send, b_own, b_recv, fin_sem,
    ready_x, ready_y,
):
    i = lax.axis_index("island")
    f = lax.axis_index("fsdp")
    y = lax.div(i, 2)
    core = lax.rem(i, 2)
    z = lax.div(f, 4)
    x = lax.rem(f, 4)
    sibling = (2 * y + (1 - core), f)
    width = error.shape[2]
    step = width // 4
    blocks = step // WIDE

    half = compressed.at[0, :, pl.ds(pl.multiple_of(8 * core, 8), 8), :]

    def share(shard):
        return compressed.at[0, shard, pl.ds(pl.multiple_of(8 * core, 8), 8), :]

    def y_peer(d):
        return (2 * lax.rem(y + d, 8) + core, f)

    barrier = pltpu.get_barrier_semaphore()

    def greet(other):
        pl.semaphore_signal(barrier, inc=1, device_id=other, device_id_type=MESH)

    @pl.loop(0, PEERS)
    def _(n):
        greet(y_peer(far(n)))
        greet((i, 4 * lax.rem(z + far(n), 8) + x))

    @pl.loop(1, 4)
    def _(n):
        greet((i, 4 * z + lax.rem(x + n, 4)))

    greet(sibling)

    loads = {}

    def load(name, src, dst):
        copy = pltpu.make_async_copy(src, dst, in_sem.at[len(loads)])
        copy.start()
        loads[name] = copy

    load("ids_s", ids, ids_s)
    load("fwd", rows_fwd, fwd)

    def columns(c):
        return pl.ds(pl.multiple_of(c * step, step), step)

    def field_loads(c):
        at = columns(c)
        return (
            pltpu.make_async_copy(error.at[0, :, at], x_v.at[:, at], field_sem.at[2 * c]),
            pltpu.make_async_copy(delta.at[0, :, at], d_v.at[:, at], field_sem.at[2 * c + 1]),
        )

    @pl.loop(0, 4)
    def _(c):
        for copy in field_loads(c):
            copy.start()

    load("ids_v", ids, ids_v)
    load("counts_v", counts, counts_v)
    load("counts_s", counts, counts_s)
    load("inv", rows_inv, inv)
    load("cols", cols_fwd, cols)
    load("param", param, p_v)
    load("velocity", velocity, v_v)

    loads["fwd"].wait()

    @pl.loop(0, 4)
    def _(c):
        at = columns(c)
        for copy in field_loads(c):
            copy.wait()
        momentum = decay_rate * x_v[:, at] + d_v[:, at].astype(F32)
        x_v[:, at] = momentum
        high, low = split(momentum)
        stack[0:64, :] = high
        stack[64:128, :] = low
        stack[128:192, :] = high
        field = jnp.dot(fwd[...], stack[...], preferred_element_type=F32)
        for j in range(blocks):
            at = pl.ds(pl.multiple_of((c * blocks + j) * SIDE, SIDE), SIDE)
            y_v[at, :] = field[:, j * WIDE:(j + 1) * WIDE]

    loads["ids_s"].wait()

    def gather(side, out):
        @pl.loop(0, 32)
        def _(o):
            for k in range(8):
                out[pl.ds(o * 8 + k, 1), :] = y_v[pl.ds(ids_s[8 * side + k, o], 1), :]

    gather(1 - core, t_sib)
    pl.semaphore_wait(barrier, 2 * PEERS + 4)

    @pl.loop(1, 4)
    def _(n):
        pl.semaphore_signal(ready_x, inc=1, device_id=(i, 4 * z + lax.rem(x + n, 4)), device_id_type=MESH)

    to_sib = pltpu.make_async_remote_copy(
        src_ref=t_sib, dst_ref=t_got, send_sem=sib_sem.at[0], recv_sem=sib_sem.at[1],
        device_id=sibling, device_id_type=MESH)
    to_sib.start()
    gather(core, t_own)
    to_sib.wait_recv()

    def sums(d):
        at = pl.ds(pl.multiple_of(lax.rem(y + d, 8) * 32, 32), 32)
        return pltpu.make_async_remote_copy(
            src_ref=part.at[at], dst_ref=got.at[d], send_sem=rs_send.at[d], recv_sem=rs_recv.at[d],
            device_id=y_peer(d), device_id_type=MESH)

    @pl.loop(0, PEERS)
    def _(n):
        at = pl.ds(pl.multiple_of(lax.rem(y + far(n), 8) * 32, 32), 32)
        part[at, :] = t_own[at, :] + t_got[at, :]
        sums(far(n)).start()

    mine = pl.ds(pl.multiple_of(y * 32, 32), 32)
    part[mine, :] = t_own[mine, :] + t_got[mine, :]
    pl.semaphore_wait(ready_x, 3)

    @pl.loop(1, 8)
    def _(d):
        pl.semaphore_signal(ready_y, inc=1, device_id=y_peer(d), device_id_type=MESH)

    loads["ids_v"].wait()
    loads["counts_v"].wait()
    loads["inv"].wait()
    listed = jnp.where(iota((16, 32), 0) < counts_v[...], ids_v[...], -1).astype(F32)
    entry = iota((32, 512), 1)
    pick = jnp.where(iota((32, 512), 0) == (entry // 8) % 32, 1.0, 0.0).astype(F32)
    spread = jnp.dot(listed, pick, precision=lax.Precision.HIGHEST, preferred_element_type=F32)
    entry = iota((16, 512), 1)
    spread = jnp.where(iota((16, 512), 0) == 8 * (entry // 256) + entry % 8, spread, 0.0)
    place = jnp.sum(spread, axis=0, keepdims=True).astype(jnp.int32)
    row_hot = jnp.where(iota((64, 512), 0) == (place & 63), 1.0, 0.0).astype(BF16)
    block_hot = jnp.where(iota((32, 512), 0) == (place >> 6), 1.0, 0.0).astype(BF16)
    mask_v[:, 0:32] = lax.dot_general(row_hot, block_hot, (((1,), (1,)), ((), ())), preferred_element_type=F32)

    def stack_block(j, values):
        at = pl.ds(j * WIDE, WIDE)
        high, low = split(values)
        stack[0:64, at] = high
        stack[64:128, at] = low
        stack[128:192, at] = high

    @pl.loop(0, 4)
    def _(c):
        at = columns(c)
        mask = pltpu.roll(mask_v[...], WIDE - c * blocks, 1)
        for j in range(blocks):
            rows = pl.ds(pl.multiple_of((c * blocks + j) * SIDE, SIDE), SIDE)
            stack_block(j, y_v[rows, :] * mask[:, j:j + 1])
        kept = jnp.dot(inv[...], stack[...], preferred_element_type=F32)
        new_error[0, :, at] = x_v[:, at] - kept

    @pl.loop(0, 32)
    def _(q):
        at = pl.ds(pl.multiple_of(q * SIDE, SIDE), SIDE)
        hot[at, :] = jnp.where(iota((SIDE, 512), 0) + q * SIDE == place, 1.0, 0.0).astype(BF16)

    loads["counts_s"].wait()
    loads["cols"].wait()

    @pl.loop(1, 8)
    def _(d):
        sums(d).wait_recv()

    total = part[mine, :]
    for d in range(1, 8):
        total = total + got[d]
    alive = []
    for r in range(4):
        live = iota((8, WIDE), 0) + 8 * core < counts_s[0, 4 * y + r]
        alive.append(jnp.where(live, total[8 * r:8 * r + 8], 0.0))
    total = jnp.concatenate(alive, axis=0)
    normed = total / jnp.sqrt(jnp.mean(total * total, axis=1, keepdims=True) + eps_value)
    ret[core, mine, :] = normed
    high, low = split(normed)
    sent[...] = (
        jnp.dot(high, cols[0], preferred_element_type=F32)
        + jnp.dot(low, cols[0], preferred_element_type=F32)
        + jnp.dot(high, cols[1], preferred_element_type=F32)
    )
    pl.semaphore_wait(ready_y, 7)

    @pl.loop(0, 4 * PEERS)
    def _(n):
        r = lax.rem(n, 4)
        pltpu.make_async_remote_copy(
            src_ref=sent.at[pl.ds(pl.multiple_of(8 * r, 8), 8)], dst_ref=share(f),
            send_sem=b_send.at[0], recv_sem=b_recv.at[0],
            device_id=(2 * lax.rem(y + far(lax.div(n, 4)), 8) + core, 4 * y + r), device_id_type=MESH).start()

    def plane(r):
        return pltpu.make_async_remote_copy(
            src_ref=sent.at[pl.ds(pl.multiple_of(8 * r, 8), 8)], dst_ref=share(f),
            send_sem=b_own.at[r], recv_sem=b_recv.at[0],
            device_id=(i, 4 * y + r), device_id_type=MESH)

    @pl.loop(0, 4)
    def _(r):
        @pl.when(4 * y + r == f)
        def _():
            at = pl.ds(pl.multiple_of(8 * r, 8), 8)
            pltpu.make_async_copy(sent.at[at], share(f), b_recv.at[0]).start()

        @pl.when(4 * y + r != f)
        def _():
            plane(r).start()

    def back(d):
        return pltpu.make_async_remote_copy(
            src_ref=ret.at[core, mine], dst_ref=ret.at[core, mine], send_sem=ag_send.at[d], recv_sem=ag_recv.at[d],
            device_id=y_peer(d), device_id_type=MESH)

    @pl.loop(0, PEERS)
    def _(n):
        back(far(n)).start()


    @pl.loop(1, 8)
    def _(d):
        back(d).wait_recv()

    relay = pltpu.make_async_remote_copy(
        src_ref=ret.at[core], dst_ref=ret.at[core], send_sem=rel_sem.at[0], recv_sem=rel_sem.at[1],
        device_id=sibling, device_id_type=MESH)
    relay.start()
    def spread(side, first):
        high, low = split(ret[side])
        both = jnp.concatenate([high, low], axis=1)
        entries = pl.ds(pl.multiple_of(side * 256, 256), 256)

        @pl.loop(0, 4)
        def _(c):
            rows = pl.ds(pl.multiple_of(c * blocks * SIDE, blocks * SIDE), blocks * SIDE)
            pieces = jnp.dot(hot[rows, entries], both, preferred_element_type=F32)
            pieces = pieces[:, :WIDE] + pieces[:, WIDE:]
            if first:
                y_v[rows, :] = pieces
            else:
                finish_update(c, y_v[rows, :] + pieces)

    def finish_update(c, pieces):
        at = columns(c)
        for j in range(blocks):
            stack_block(j, pieces[j * SIDE:(j + 1) * SIDE])
        update = jnp.dot(inv[...], stack[...], preferred_element_type=F32)
        moved = nesterov * v_v[:, at].astype(F32) + update
        new_param[:, at] = (p_v[:, at].astype(F32) - outer_rate * (update + nesterov * moved)).astype(BF16)
        new_velocity[:, at] = moved.astype(BF16)

    spread(core, True)

    pltpu.make_async_copy(half, half, b_recv.at[0]).wait()
    finish = pltpu.make_async_remote_copy(
        src_ref=half, dst_ref=half, send_sem=fin_sem.at[0], recv_sem=fin_sem.at[1],
        device_id=sibling, device_id_type=MESH)
    finish.start()
    loads["param"].wait()
    loads["velocity"].wait()
    relay.wait_recv()
    spread(1 - core, False)
    finish.wait_recv()

    to_sib.wait_send()
    relay.wait_send()
    finish.wait_send()

    @pl.loop(1, 8)
    def _(d):
        sums(d).wait_send()
        back(d).wait_send()

    out_rows = pl.ds(0, 28 * 8)
    pltpu.make_async_copy(part.at[out_rows], part.at[out_rows], b_send.at[0]).wait()

    @pl.loop(0, 4)
    def _(r):
        @pl.when(4 * y + r != f)
        def _():
            plane(r).wait_send()


def settle(*refs):
    sources, targets, sem = refs[:4], refs[4:8], refs[8]
    copies = [pltpu.make_async_copy(a, b, sem.at[n]) for n, (a, b) in enumerate(zip(sources, targets))]
    for copy in copies:
        copy.start()
    for copy in copies:
        copy.wait()


def shards(delta, error, param, velocity, piece_ids, piece_counts):
    table = cosine_table(SIDE)
    high, low = halves(table)
    rows_fwd = jnp.asarray(np.concatenate([high, high, low], axis=1))
    rows_inv = jnp.asarray(np.concatenate([high.T, high.T, low.T], axis=1))
    cols_fwd = jnp.asarray(np.stack(halves(np.kron(np.eye(2), table.T))))
    rows, width = param.shape
    any_space = pl.BlockSpec(memory_space=pl.ANY)
    dma = pltpu.SemaphoreType.DMA
    step = width // 4
    results = pl.pallas_call(
        kernel,
        out_shape=(
            pltpu.VMEM(error.shape, F32),
            pltpu.VMEM(param.shape, BF16),
            pltpu.VMEM(param.shape, BF16),
            pltpu.VMEM((1, 32, 16, WIDE), F32),
        ),
        in_specs=[any_space] * 9,
        out_specs=(pl.BlockSpec(memory_space=pltpu.VMEM),) * 4,
        scratch_shapes=[
            pltpu.SMEM((16, 32), jnp.int32),
            pltpu.SMEM((1, 32), jnp.int32),
            pltpu.VMEM((16, 32), jnp.int32),
            pltpu.VMEM((1, 32), jnp.int32),
            pltpu.VMEM((64, 192), BF16),
            pltpu.VMEM((64, 192), BF16),
            pltpu.VMEM((2, 128, 128), BF16),
            pltpu.VMEM((rows, width), BF16),
            pltpu.VMEM((rows, width), F32),
            pltpu.VMEM((rows, width), BF16),
            pltpu.VMEM((rows, width), BF16),
            pltpu.VMEM((2048, WIDE), F32),
            pltpu.VMEM((192, step), BF16),
            pltpu.VMEM((2048, 512), BF16),
            pltpu.VMEM((64, 128), F32),
            pltpu.VMEM((256, WIDE), F32),
            pltpu.VMEM((256, WIDE), F32),
            pltpu.VMEM((256, WIDE), F32),
            pltpu.VMEM((256, WIDE), F32),
            pltpu.VMEM((8, 32, WIDE), F32),
            pltpu.VMEM((2, 256, WIDE), F32),
            pltpu.VMEM((32, WIDE), F32),
            dma((20,)),
            dma((8,)),
            dma((2,)),
            dma((8,)),
            dma((8,)),
            dma((8,)),
            dma((8,)),
            dma((2,)),
            dma((1,)),
            dma((4,)),
            dma((1,)),
            dma((2,)),
            pltpu.SemaphoreType.REGULAR,
            pltpu.SemaphoreType.REGULAR,
        ],
        compiler_params=pltpu.CompilerParams(
            collective_id=0, has_side_effects=True, vmem_limit_bytes=56 << 20),
        name="sync",
    )(delta, error, param, velocity, piece_ids[0].T, piece_counts, rows_fwd, rows_inv, cols_fwd)
    results = [pltpu.with_memory_space_constraint(a, pltpu.VMEM) for a in results]
    return pl.pallas_call(
        settle,
        out_shape=tuple(pltpu.HBM(a.shape, a.dtype) for a in results),
        in_specs=[pl.BlockSpec(memory_space=pltpu.VMEM)] * 4,
        out_specs=(pl.BlockSpec(memory_space=pltpu.HBM),) * 4,
        scratch_shapes=[dma((4,))],
        name="settle",
    )(*results)


def solution(mesh):
    in_specs = (
        P("island", "fsdp", None),
        P("island", "fsdp", None),
        P("fsdp", None),
        P("fsdp", None),
        P("fsdp", None, None),
        P("fsdp", None),
    )
    out_specs = (
        P("island", "fsdp", None),
        P("fsdp", None),
        P("fsdp", None),
        P("fsdp", None, None, None),
    )
    return jax.shard_map(shards, mesh=mesh, in_specs=in_specs, out_specs=out_specs, check_vma=False)
```

```python
import functools
import math

import jax
import jax.numpy as jnp
import ml_dtypes
import numpy as np
from jax import lax
from jax.experimental import pallas as pl
from jax.experimental.pallas import tpu as pltpu
from jax.sharding import PartitionSpec as P

MESH = pl.DeviceIdType.MESH
F32 = jnp.float32
BF16 = jnp.bfloat16

decay_rate = 0.9
outer_rate = 0.7
nesterov = 0.9
eps_value = 1e-06

SIDE = 64
WIDE = 128
PEERS = 7


def far(n):
    return 4 + (1 - 2 * lax.rem(n, 2)) * lax.div(n + 1, 2)


def cosine_table(side):
    freq = np.arange(side, dtype=np.float64)[:, None]
    place = np.arange(side, dtype=np.float64)[None, :]
    scale = np.where(freq == 0, math.sqrt(1.0 / side), math.sqrt(2.0 / side))
    return scale * np.cos(math.pi * (2.0 * place + 1.0) * freq / (2.0 * side))


def halves(table):
    high = table.astype(np.float32).astype(ml_dtypes.bfloat16)
    low = (table - high.astype(np.float64)).astype(ml_dtypes.bfloat16)
    return high, low


def split(values):
    high = values.astype(BF16)
    low = (values - high.astype(F32)).astype(BF16)
    return high, low


def iota(shape, dim):
    return lax.broadcasted_iota(jnp.int32, shape, dim)


def kernel(
    delta, error, param, velocity, ids, counts, rows_fwd, rows_inv, cols_fwd,
    new_error, new_param, new_velocity, compressed,
    ids_s, counts_s, ids_v, counts_v, fwd, inv, cols, d_v, x_v, p_v, v_v, y_v, stack, basis_high, basis_low, mask_v, block_v,
    t_sib, t_own, t_got, part, got, ret, sent,
    in_sem, field_sem, sib_send, sib_recv, rs_send, rs_recv, ag_send, ag_recv, rel_sem, b_send, b_own, b_recv, fin_sem,
    ready_x, ready_y,
):
    i = lax.axis_index("island")
    f = lax.axis_index("fsdp")
    y = lax.div(i, 2)
    core = lax.rem(i, 2)
    z = lax.div(f, 4)
    x = lax.rem(f, 4)
    sibling = (2 * y + (1 - core), f)
    width = error.shape[2]
    step = width // 4
    blocks = step // WIDE

    half = compressed.at[0, :, pl.ds(pl.multiple_of(8 * core, 8), 8), :]

    def share(shard):
        return compressed.at[0, shard, pl.ds(pl.multiple_of(8 * core, 8), 8), :]

    def y_peer(d):
        return (2 * lax.rem(y + d, 8) + core, f)

    barrier = pltpu.get_barrier_semaphore()

    def greet(other):
        pl.semaphore_signal(barrier, inc=1, device_id=other, device_id_type=MESH)

    @pl.loop(0, PEERS)
    def _(n):
        greet(y_peer(far(n)))
        greet((i, 4 * lax.rem(z + far(n), 8) + x))

    @pl.loop(1, 4)
    def _(n):
        greet((i, 4 * z + lax.rem(x + n, 4)))

    greet(sibling)

    loads = {}

    def load(name, src, dst):
        copy = pltpu.make_async_copy(src, dst, in_sem.at[len(loads)])
        copy.start()
        loads[name] = copy

    load("ids_s", ids, ids_s)
    load("fwd", rows_fwd, fwd)

    def columns(c):
        return pl.ds(pl.multiple_of(c * step, step), step)

    def field_loads(c):
        at = columns(c)
        return (
            pltpu.make_async_copy(error.at[0, :, at], x_v.at[:, at], field_sem.at[2 * c]),
            pltpu.make_async_copy(delta.at[0, :, at], d_v.at[:, at], field_sem.at[2 * c + 1]),
        )

    @pl.loop(0, 4)
    def _(c):
        for copy in field_loads(c):
            copy.start()

    load("ids_v", ids, ids_v)
    load("counts_v", counts, counts_v)
    load("counts_s", counts, counts_s)
    load("inv", rows_inv, inv)
    load("cols", cols_fwd, cols)

    loads["fwd"].wait()

    @pl.loop(0, 4)
    def _(c):
        at = columns(c)
        for copy in field_loads(c):
            copy.wait()
        momentum = decay_rate * x_v[:, at] + d_v[:, at].astype(F32)
        x_v[:, at] = momentum
        high, low = split(momentum)
        stack[0:64, :] = high
        stack[64:128, :] = low
        stack[128:192, :] = high
        field = jnp.dot(fwd[...], stack[...], preferred_element_type=F32)
        for j in range(blocks):
            at = pl.ds(pl.multiple_of((c * blocks + j) * SIDE, SIDE), SIDE)
            y_v[at, :] = field[:, j * WIDE:(j + 1) * WIDE]

    loads["ids_s"].wait()

    def gather(side, out, site):
        @pl.loop(0, 4)
        def _(r):
            for k in range(8):
                row = ids_s[8 * side + k, 4 * site + r]
                out[pl.ds(site * 32 + r * 8 + k, 1), :] = y_v[pl.ds(row, 1), :]

    def site_of(n):
        return lax.rem(y + lax.select(n == PEERS, 0, far(n)), 8)

    def rows_of(site):
        return pl.ds(pl.multiple_of(site * 32, 32), 32)

    def exchange(n):
        at = rows_of(site_of(n))
        return pltpu.make_async_remote_copy(
            src_ref=t_sib.at[at], dst_ref=t_got.at[at], send_sem=sib_send.at[n], recv_sem=sib_recv.at[n],
            device_id=sibling, device_id_type=MESH)

    @pl.loop(0, 8)
    def _(n):
        gather(1 - core, t_sib, site_of(n))

    pl.semaphore_wait(barrier, 2 * PEERS + 4)

    @pl.loop(0, 8)
    def _(n):
        exchange(n).start()

    @pl.loop(1, 4)
    def _(n):
        pl.semaphore_signal(ready_x, inc=1, device_id=(i, 4 * z + lax.rem(x + n, 4)), device_id_type=MESH)

    @pl.loop(0, 8)
    def _(n):
        gather(core, t_own, site_of(n))

    def sums(d):
        at = rows_of(lax.rem(y + d, 8))
        return pltpu.make_async_remote_copy(
            src_ref=part.at[at], dst_ref=got.at[d], send_sem=rs_send.at[d], recv_sem=rs_recv.at[d],
            device_id=y_peer(d), device_id_type=MESH)

    @pl.loop(0, PEERS)
    def _(n):
        at = rows_of(site_of(n))
        exchange(n).wait_recv()
        part[at, :] = t_own[at, :] + t_got[at, :]
        sums(far(n)).start()

    exchange(PEERS).wait_recv()
    mine = pl.ds(pl.multiple_of(y * 32, 32), 32)
    part[mine, :] = t_own[mine, :] + t_got[mine, :]
    pl.semaphore_wait(ready_x, 3)

    @pl.loop(1, 8)
    def _(d):
        pl.semaphore_signal(ready_y, inc=1, device_id=y_peer(d), device_id_type=MESH)

    load("param", param, p_v)
    load("velocity", velocity, v_v)

    loads["ids_v"].wait()
    loads["counts_v"].wait()
    loads["inv"].wait()
    listed = jnp.where(iota((16, 32), 0) < counts_v[...], ids_v[...], -1).astype(F32)
    entry = iota((32, 512), 1)
    pick = jnp.where(iota((32, 512), 0) == (entry // 8) % 32, 1.0, 0.0).astype(F32)
    spread = jnp.dot(listed, pick, precision=lax.Precision.HIGHEST, preferred_element_type=F32)
    entry = iota((16, 512), 1)
    spread = jnp.where(iota((16, 512), 0) == 8 * (entry // 256) + entry % 8, spread, 0.0)
    place = jnp.sum(spread, axis=0, keepdims=True).astype(jnp.int32)
    row_hot = jnp.where(iota((64, 512), 0) == (place & 63), 1.0, 0.0).astype(BF16)
    block_hot = jnp.where(iota((32, 512), 0) == (place >> 6), 1.0, 0.0).astype(BF16)
    mask_v[:, 0:32] = lax.dot_general(row_hot, block_hot, (((1,), (1,)), ((), ())), preferred_element_type=F32)
    block_v[...] = block_hot.astype(F32)
    entry_high = jnp.dot(inv[:, 0:64], row_hot, preferred_element_type=F32)
    entry_low = jnp.dot(inv[:, 128:192], row_hot, preferred_element_type=F32)

    @pl.loop(0, 32)
    def _(q):
        at = pl.ds(pl.multiple_of(q * SIDE, SIDE), SIDE)
        here = block_v[pl.ds(q, 1), :]
        basis_high[at, :] = (entry_high * here).astype(BF16)
        basis_low[at, :] = (entry_low * here).astype(BF16)

    def stack_block(j, values):
        at = pl.ds(j * WIDE, WIDE)
        high, low = split(values)
        stack[0:64, at] = high
        stack[64:128, at] = low
        stack[128:192, at] = high

    @pl.loop(0, 4)
    def _(c):
        at = columns(c)
        mask = pltpu.roll(mask_v[...], WIDE - c * blocks, 1)
        for j in range(blocks):
            rows = pl.ds(pl.multiple_of((c * blocks + j) * SIDE, SIDE), SIDE)
            stack_block(j, y_v[rows, :] * mask[:, j:j + 1])
        kept = jnp.dot(inv[...], stack[...], preferred_element_type=F32)
        new_error[0, :, at] = x_v[:, at] - kept

    loads["counts_s"].wait()
    loads["cols"].wait()

    @pl.loop(1, 8)
    def _(d):
        sums(d).wait_recv()

    total = part[mine, :]
    for d in range(1, 8):
        total = total + got[d]
    alive = []
    for r in range(4):
        live = iota((8, WIDE), 0) + 8 * core < counts_s[0, 4 * y + r]
        alive.append(jnp.where(live, total[8 * r:8 * r + 8], 0.0))
    total = jnp.concatenate(alive, axis=0)
    high, low = split(total)
    spectrum = (
        jnp.dot(high, cols[0], preferred_element_type=F32)
        + jnp.dot(low, cols[0], preferred_element_type=F32)
        + jnp.dot(high, cols[1], preferred_element_type=F32)
    )
    level = jnp.sqrt(jnp.mean(total * total, axis=1, keepdims=True) + eps_value)
    sent[...] = spectrum / level
    ret[core, mine, :] = total / level
    pl.semaphore_wait(ready_y, 7)

    def to_owner(site, r, sem):
        return pltpu.make_async_remote_copy(
            src_ref=sent.at[pl.ds(pl.multiple_of(8 * r, 8), 8)], dst_ref=share(f), send_sem=sem, recv_sem=b_recv.at[0],
            device_id=(2 * site + core, 4 * y + r), device_id_type=MESH)

    def back(d):
        return pltpu.make_async_remote_copy(
            src_ref=ret.at[core, mine], dst_ref=ret.at[core, mine], send_sem=ag_send.at[d], recv_sem=ag_recv.at[d],
            device_id=y_peer(d), device_id_type=MESH)

    @pl.loop(0, 4)
    def _(r):
        for n in range(PEERS):
            to_owner(lax.rem(y + (4, 3, 5, 2, 6, 1, 7)[n], 8), r, b_send.at[0]).start()

    @pl.loop(0, 4)
    def _(r):
        @pl.when(4 * y + r == f)
        def _():
            at = pl.ds(pl.multiple_of(8 * r, 8), 8)
            pltpu.make_async_copy(sent.at[at], share(f), b_recv.at[0]).start()

        @pl.when(4 * y + r != f)
        def _():
            to_owner(y, r, b_own.at[r]).start()

    @pl.loop(0, PEERS)
    def _(n):
        back(far(n)).start()


    @pl.loop(1, 8)
    def _(d):
        back(d).wait_recv()

    relay = pltpu.make_async_remote_copy(
        src_ref=ret.at[core], dst_ref=ret.at[core], send_sem=rel_sem.at[0], recv_sem=rel_sem.at[1],
        device_id=sibling, device_id_type=MESH)
    relay.start()
    def spread(side, first):
        high, low = split(ret[side])
        both = jnp.concatenate([high, low], axis=1)
        entries = pl.ds(pl.multiple_of(side * 256, 256), 256)

        @pl.loop(0, 4)
        def _(c):
            rows = pl.ds(pl.multiple_of(c * blocks * SIDE, blocks * SIDE), blocks * SIDE)
            fields = jnp.dot(basis_high[rows, entries], both, preferred_element_type=F32)
            field = fields[:, :WIDE] + fields[:, WIDE:]
            field = field + jnp.dot(basis_low[rows, entries], high, preferred_element_type=F32)
            if first:
                y_v[rows, :] = field
            else:
                field = y_v[rows, :] + field
                for j in range(blocks):
                    at = pl.ds(pl.multiple_of((c * blocks + j) * WIDE, WIDE), WIDE)
                    update = field[j * SIDE:(j + 1) * SIDE]
                    moved = nesterov * v_v[:, at].astype(F32) + update
                    step_back = outer_rate * (update + nesterov * moved)
                    new_param[:, at] = (p_v[:, at].astype(F32) - step_back).astype(BF16)
                    new_velocity[:, at] = moved.astype(BF16)

    spread(core, True)

    pltpu.make_async_copy(half, half, b_recv.at[0]).wait()
    finish = pltpu.make_async_remote_copy(
        src_ref=half, dst_ref=half, send_sem=fin_sem.at[0], recv_sem=fin_sem.at[1],
        device_id=sibling, device_id_type=MESH)
    finish.start()
    loads["param"].wait()
    loads["velocity"].wait()
    relay.wait_recv()
    spread(1 - core, False)
    finish.wait_recv()


    @pl.loop(0, 8)
    def _(n):
        exchange(n).wait_send()

    relay.wait_send()
    finish.wait_send()

    @pl.loop(1, 8)
    def _(d):
        sums(d).wait_send()
        back(d).wait_send()

    out_rows = pl.ds(0, 28 * 8)
    pltpu.make_async_copy(part.at[out_rows], part.at[out_rows], b_send.at[0]).wait()

    @pl.loop(0, 4)
    def _(r):
        @pl.when(4 * y + r != f)
        def _():
            to_owner(y, r, b_own.at[r]).wait_send()


def settle(*refs):
    sources, targets, sem = refs[:4], refs[4:8], refs[8]
    copies = [pltpu.make_async_copy(a, b, sem.at[n]) for n, (a, b) in enumerate(zip(sources, targets))]
    for copy in copies:
        copy.start()
    for copy in copies:
        copy.wait()


def shards(delta, error, param, velocity, piece_ids, piece_counts):
    table = cosine_table(SIDE)
    high, low = halves(table)
    rows_fwd = jnp.asarray(np.concatenate([high, high, low], axis=1))
    rows_inv = jnp.asarray(np.concatenate([high.T, high.T, low.T], axis=1))
    cols_fwd = jnp.asarray(np.stack(halves(np.kron(np.eye(2), table.T))))
    rows, width = param.shape
    any_space = pl.BlockSpec(memory_space=pl.ANY)
    dma = pltpu.SemaphoreType.DMA
    step = width // 4
    results = pl.pallas_call(
        kernel,
        out_shape=(
            pltpu.VMEM(error.shape, F32),
            pltpu.VMEM(param.shape, BF16),
            pltpu.VMEM(param.shape, BF16),
            pltpu.VMEM((1, 32, 16, WIDE), F32),
        ),
        in_specs=[any_space] * 9,
        out_specs=(pl.BlockSpec(memory_space=pltpu.VMEM),) * 4,
        scratch_shapes=[
            pltpu.SMEM((16, 32), jnp.int32),
            pltpu.SMEM((1, 32), jnp.int32),
            pltpu.VMEM((16, 32), jnp.int32),
            pltpu.VMEM((1, 32), jnp.int32),
            pltpu.VMEM((64, 192), BF16),
            pltpu.VMEM((64, 192), BF16),
            pltpu.VMEM((2, 128, 128), BF16),
            pltpu.VMEM((rows, width), BF16),
            pltpu.VMEM((rows, width), F32),
            pltpu.VMEM((rows, width), BF16),
            pltpu.VMEM((rows, width), BF16),
            pltpu.VMEM((2048, WIDE), F32),
            pltpu.VMEM((192, step), BF16),
            pltpu.VMEM((2048, 512), BF16),
            pltpu.VMEM((2048, 512), BF16),
            pltpu.VMEM((64, 128), F32),
            pltpu.VMEM((32, 512), F32),
            pltpu.VMEM((256, WIDE), F32),
            pltpu.VMEM((256, WIDE), F32),
            pltpu.VMEM((256, WIDE), F32),
            pltpu.VMEM((256, WIDE), F32),
            pltpu.VMEM((8, 32, WIDE), F32),
            pltpu.VMEM((2, 256, WIDE), F32),
            pltpu.VMEM((32, WIDE), F32),
            dma((20,)),
            dma((8,)),
            dma((8,)),
            dma((8,)),
            dma((8,)),
            dma((8,)),
            dma((8,)),
            dma((8,)),
            dma((2,)),
            dma((1,)),
            dma((4,)),
            dma((1,)),
            dma((2,)),
            pltpu.SemaphoreType.REGULAR,
            pltpu.SemaphoreType.REGULAR,
        ],
        compiler_params=pltpu.CompilerParams(
            collective_id=0, has_side_effects=True, vmem_limit_bytes=56 << 20),
        name="sync",
    )(delta, error, param, velocity, piece_ids[0].T, piece_counts, rows_fwd, rows_inv, cols_fwd)
    results = [pltpu.with_memory_space_constraint(a, pltpu.VMEM) for a in results]
    return pl.pallas_call(
        settle,
        out_shape=tuple(pltpu.HBM(a.shape, a.dtype) for a in results),
        in_specs=[pl.BlockSpec(memory_space=pltpu.VMEM)] * 4,
        out_specs=(pl.BlockSpec(memory_space=pltpu.HBM),) * 4,
        scratch_shapes=[dma((4,))],
        name="settle",
    )(*results)


def solution(mesh):
    in_specs = (
        P("island", "fsdp", None),
        P("island", "fsdp", None),
        P("fsdp", None),
        P("fsdp", None),
        P("fsdp", None, None),
        P("fsdp", None),
    )
    out_specs = (
        P("island", "fsdp", None),
        P("fsdp", None),
        P("fsdp", None),
        P("fsdp", None, None, None),
    )
    return jax.shard_map(shards, mesh=mesh, in_specs=in_specs, out_specs=out_specs, check_vma=False)
```

```python
import functools
import math

import jax
import jax.numpy as jnp
import ml_dtypes
import numpy as np
from jax import lax
from jax.experimental import pallas as pl
from jax.experimental.pallas import tpu as pltpu
from jax.sharding import PartitionSpec as P

MESH = pl.DeviceIdType.MESH
F32 = jnp.float32
BF16 = jnp.bfloat16

decay_rate = 0.9
outer_rate = 0.7
nesterov = 0.9
eps_value = 1e-06

SIDE = 64
WIDE = 128
PEERS = 7


def far(n):
    return 4 + (1 - 2 * lax.rem(n, 2)) * lax.div(n + 1, 2)


def cosine_table(side):
    freq = np.arange(side, dtype=np.float64)[:, None]
    place = np.arange(side, dtype=np.float64)[None, :]
    scale = np.where(freq == 0, math.sqrt(1.0 / side), math.sqrt(2.0 / side))
    return scale * np.cos(math.pi * (2.0 * place + 1.0) * freq / (2.0 * side))


def halves(table):
    high = table.astype(np.float32).astype(ml_dtypes.bfloat16)
    low = (table - high.astype(np.float64)).astype(ml_dtypes.bfloat16)
    return high, low


def split(values):
    high = values.astype(BF16)
    low = (values - high.astype(F32)).astype(BF16)
    return high, low


def iota(shape, dim):
    return lax.broadcasted_iota(jnp.int32, shape, dim)


def kernel(
    delta, error, param, velocity, ids, counts, rows_fwd, rows_inv, cols_fwd,
    new_error, new_param, new_velocity, compressed,
    ids_s, counts_s, ids_v, counts_v, fwd, inv, cols, d_v, x_v, p_v, v_v, y_v, stack, basis_high, basis_low, mask_v, block_v,
    t_sib, t_own, t_got, part, got, ret, sent,
    in_sem, field_sem, sib_send, sib_recv, rs_send, rs_recv, ag_send, ag_recv, rel_sem, b_send, b_own, b_recv, fin_sem,
    ready_x, ready_y,
):
    i = lax.axis_index("island")
    f = lax.axis_index("fsdp")
    y = lax.div(i, 2)
    core = lax.rem(i, 2)
    z = lax.div(f, 4)
    x = lax.rem(f, 4)
    sibling = (2 * y + (1 - core), f)
    width = error.shape[2]
    step = width // 4
    blocks = step // WIDE

    half = compressed.at[0, :, pl.ds(pl.multiple_of(8 * core, 8), 8), :]

    def share(shard):
        return compressed.at[0, shard, pl.ds(pl.multiple_of(8 * core, 8), 8), :]

    def y_peer(d):
        return (2 * lax.rem(y + d, 8) + core, f)

    barrier = pltpu.get_barrier_semaphore()

    def greet(other):
        pl.semaphore_signal(barrier, inc=1, device_id=other, device_id_type=MESH)

    @pl.loop(0, PEERS)
    def _(n):
        greet(y_peer(far(n)))
        greet((i, 4 * lax.rem(z + far(n), 8) + x))

    @pl.loop(1, 4)
    def _(n):
        greet((i, 4 * z + lax.rem(x + n, 4)))

    opposite = (2 * lax.rem(y + 4, 8) + 1 - core, f)
    greet(opposite)
    greet(sibling)

    loads = {}

    def load(name, src, dst):
        copy = pltpu.make_async_copy(src, dst, in_sem.at[len(loads)])
        copy.start()
        loads[name] = copy

    load("ids_s", ids, ids_s)
    load("fwd", rows_fwd, fwd)

    def columns(c):
        return pl.ds(pl.multiple_of(c * step, step), step)

    def field_loads(c):
        at = columns(c)
        return (
            pltpu.make_async_copy(error.at[0, :, at], x_v.at[:, at], field_sem.at[2 * c]),
            pltpu.make_async_copy(delta.at[0, :, at], d_v.at[:, at], field_sem.at[2 * c + 1]),
        )

    @pl.loop(0, 4)
    def _(c):
        for copy in field_loads(c):
            copy.start()

    load("ids_v", ids, ids_v)
    load("counts_v", counts, counts_v)
    load("counts_s", counts, counts_s)
    load("inv", rows_inv, inv)
    load("cols", cols_fwd, cols)

    loads["fwd"].wait()

    @pl.loop(0, 4)
    def _(c):
        at = columns(c)
        for copy in field_loads(c):
            copy.wait()
        momentum = decay_rate * x_v[:, at] + d_v[:, at].astype(F32)
        x_v[:, at] = momentum
        high, low = split(momentum)
        stack[0:64, :] = high
        stack[64:128, :] = low
        stack[128:192, :] = high
        field = jnp.dot(fwd[...], stack[...], preferred_element_type=F32)
        for j in range(blocks):
            at = pl.ds(pl.multiple_of((c * blocks + j) * SIDE, SIDE), SIDE)
            y_v[at, :] = field[:, j * WIDE:(j + 1) * WIDE]

    loads["ids_s"].wait()

    def gather(side, out, site):
        @pl.loop(0, 4)
        def _(r):
            for k in range(8):
                row = ids_s[8 * side + k, 4 * site + r]
                out[pl.ds(site * 32 + r * 8 + k, 1), :] = y_v[pl.ds(row, 1), :]

    def site_of(n):
        return lax.rem(y + lax.select(n == PEERS, 0, far(n)), 8)

    def rows_of(site):
        return pl.ds(pl.multiple_of(site * 32, 32), 32)

    def exchange(n):
        at = rows_of(site_of(n))
        return pltpu.make_async_remote_copy(
            src_ref=t_sib.at[at], dst_ref=t_got.at[at], send_sem=sib_send.at[n], recv_sem=sib_recv.at[n],
            device_id=sibling, device_id_type=MESH)

    @pl.loop(0, 8)
    def _(n):
        gather(1 - core, t_sib, site_of(n))

    @pl.loop(0, 8)
    def _(n):
        gather(core, t_own, site_of(n))

    pl.semaphore_wait(barrier, 2 * PEERS + 5)

    def direct(source, other, slot):
        return pltpu.make_async_remote_copy(
            src_ref=source.at[rows_of(site_of(0))], dst_ref=got.at[slot],
            send_sem=rs_send.at[slot], recv_sem=rs_recv.at[slot], device_id=other, device_id_type=MESH)

    direct(t_own, y_peer(4), 4).start()
    direct(t_sib, opposite, 0).start()

    @pl.loop(1, 8)
    def _(n):
        exchange(n).start()

    @pl.loop(1, 4)
    def _(n):
        pl.semaphore_signal(ready_x, inc=1, device_id=(i, 4 * z + lax.rem(x + n, 4)), device_id_type=MESH)

    def sums(d):
        at = rows_of(lax.rem(y + d, 8))
        return pltpu.make_async_remote_copy(
            src_ref=part.at[at], dst_ref=got.at[d], send_sem=rs_send.at[d], recv_sem=rs_recv.at[d],
            device_id=y_peer(d), device_id_type=MESH)

    @pl.loop(1, PEERS)
    def _(n):
        at = rows_of(site_of(n))
        exchange(n).wait_recv()
        part[at, :] = t_own[at, :] + t_got[at, :]
        sums(far(n)).start()

    exchange(PEERS).wait_recv()
    mine = pl.ds(pl.multiple_of(y * 32, 32), 32)
    part[mine, :] = t_own[mine, :] + t_got[mine, :]
    pl.semaphore_wait(ready_x, 3)

    @pl.loop(1, 8)
    def _(d):
        pl.semaphore_signal(ready_y, inc=1, device_id=y_peer(d), device_id_type=MESH)

    load("param", param, p_v)
    load("velocity", velocity, v_v)

    loads["ids_v"].wait()
    loads["counts_v"].wait()
    loads["inv"].wait()
    listed = jnp.where(iota((16, 32), 0) < counts_v[...], ids_v[...], -1).astype(F32)
    entry = iota((32, 512), 1)
    pick = jnp.where(iota((32, 512), 0) == (entry // 8) % 32, 1.0, 0.0).astype(F32)
    spread = jnp.dot(listed, pick, precision=lax.Precision.HIGHEST, preferred_element_type=F32)
    entry = iota((16, 512), 1)
    spread = jnp.where(iota((16, 512), 0) == 8 * (entry // 256) + entry % 8, spread, 0.0)
    place = jnp.sum(spread, axis=0, keepdims=True).astype(jnp.int32)
    row_hot = jnp.where(iota((64, 512), 0) == (place & 63), 1.0, 0.0).astype(BF16)
    block_hot = jnp.where(iota((32, 512), 0) == (place >> 6), 1.0, 0.0).astype(BF16)
    mask_v[:, 0:32] = lax.dot_general(row_hot, block_hot, (((1,), (1,)), ((), ())), preferred_element_type=F32)
    block_v[...] = block_hot.astype(F32)
    entry_high = jnp.dot(inv[:, 0:64], row_hot, preferred_element_type=F32)
    entry_low = jnp.dot(inv[:, 128:192], row_hot, preferred_element_type=F32)

    @pl.loop(0, 32)
    def _(q):
        at = pl.ds(pl.multiple_of(q * SIDE, SIDE), SIDE)
        here = block_v[pl.ds(q, 1), :]
        basis_high[at, :] = (entry_high * here).astype(BF16)
        basis_low[at, :] = (entry_low * here).astype(BF16)

    def stack_block(j, values):
        at = pl.ds(j * WIDE, WIDE)
        high, low = split(values)
        stack[0:64, at] = high
        stack[64:128, at] = low
        stack[128:192, at] = high

    @pl.loop(0, 4)
    def _(c):
        at = columns(c)
        mask = pltpu.roll(mask_v[...], WIDE - c * blocks, 1)
        for j in range(blocks):
            rows = pl.ds(pl.multiple_of((c * blocks + j) * SIDE, SIDE), SIDE)
            stack_block(j, y_v[rows, :] * mask[:, j:j + 1])
        kept = jnp.dot(inv[...], stack[...], preferred_element_type=F32)
        new_error[0, :, at] = x_v[:, at] - kept

    loads["counts_s"].wait()
    loads["cols"].wait()

    @pl.loop(0, 8)
    def _(d):
        sums(d).wait_recv()

    total = part[mine, :]
    for d in range(8):
        total = total + got[d]
    alive = []
    for r in range(4):
        live = iota((8, WIDE), 0) + 8 * core < counts_s[0, 4 * y + r]
        alive.append(jnp.where(live, total[8 * r:8 * r + 8], 0.0))
    total = jnp.concatenate(alive, axis=0)
    high, low = split(total)
    spectrum = jnp.dot(jnp.concatenate([high, low, high], axis=1), cols[...], preferred_element_type=F32)
    scale = 1.0 / jnp.sqrt(jnp.mean(total * total, axis=1, keepdims=True) + eps_value)
    sent[...] = spectrum * scale
    ret[core, mine, :] = total * scale
    pl.semaphore_wait(ready_y, 7)

    def to_owner(site, r, sem):
        return pltpu.make_async_remote_copy(
            src_ref=sent.at[pl.ds(pl.multiple_of(8 * r, 8), 8)], dst_ref=share(f), send_sem=sem, recv_sem=b_recv.at[0],
            device_id=(2 * site + core, 4 * y + r), device_id_type=MESH)

    def back(d):
        return pltpu.make_async_remote_copy(
            src_ref=ret.at[core, mine], dst_ref=ret.at[core, mine], send_sem=ag_send.at[d], recv_sem=ag_recv.at[d],
            device_id=y_peer(d), device_id_type=MESH)

    @pl.loop(0, 4)
    def _(r):
        for n in range(PEERS):
            to_owner(lax.rem(y + (4, 3, 5, 2, 6, 1, 7)[n], 8), r, b_send.at[0]).start()

    @pl.loop(0, 4)
    def _(r):
        @pl.when(4 * y + r == f)
        def _():
            at = pl.ds(pl.multiple_of(8 * r, 8), 8)
            pltpu.make_async_copy(sent.at[at], share(f), b_recv.at[0]).start()

        @pl.when(4 * y + r != f)
        def _():
            to_owner(y, r, b_own.at[r]).start()

    @pl.loop(0, PEERS)
    def _(n):
        back(far(n)).start()


    def relay(d):
        at = pl.ds(pl.multiple_of(lax.rem(y + 8 - d, 8) * 32, 32), 32)
        return pltpu.make_async_remote_copy(
            src_ref=ret.at[core, at], dst_ref=ret.at[core, at], send_sem=rel_sem.at[0], recv_sem=rel_sem.at[1],
            device_id=sibling, device_id_type=MESH)

    relay(0).start()

    @pl.loop(0, PEERS)
    def _(n):
        d = far(PEERS - 1 - n)
        back(d).wait_recv()
        relay(d).start()

    def spread(side, first):
        high, low = split(ret[side])
        both = jnp.concatenate([high, low], axis=1)
        entries = pl.ds(pl.multiple_of(side * 256, 256), 256)

        @pl.loop(0, 4)
        def _(c):
            rows = pl.ds(pl.multiple_of(c * blocks * SIDE, blocks * SIDE), blocks * SIDE)
            fields = jnp.dot(basis_high[rows, entries], both, preferred_element_type=F32)
            field = fields[:, :WIDE] + fields[:, WIDE:]
            field = field + jnp.dot(basis_low[rows, entries], high, preferred_element_type=F32)
            if first:
                y_v[rows, :] = field
            else:
                field = y_v[rows, :] + field
                for j in range(blocks):
                    at = pl.ds(pl.multiple_of((c * blocks + j) * WIDE, WIDE), WIDE)
                    update = field[j * SIDE:(j + 1) * SIDE]
                    moved = nesterov * v_v[:, at].astype(F32) + update
                    step_back = outer_rate * (update + nesterov * moved)
                    new_param[:, at] = (p_v[:, at].astype(F32) - step_back).astype(BF16)
                    new_velocity[:, at] = moved.astype(BF16)

    spread(core, True)

    pltpu.make_async_copy(half, half, b_recv.at[0]).wait()
    finish = pltpu.make_async_remote_copy(
        src_ref=half, dst_ref=half, send_sem=fin_sem.at[0], recv_sem=fin_sem.at[1],
        device_id=sibling, device_id_type=MESH)
    finish.start()
    loads["param"].wait()
    loads["velocity"].wait()
    pltpu.make_async_copy(ret.at[core], ret.at[core], rel_sem.at[1]).wait()
    spread(1 - core, False)
    finish.wait_recv()


    @pl.loop(1, 8)
    def _(n):
        exchange(n).wait_send()

    sums(0).wait_send()
    pltpu.make_async_copy(ret.at[core], ret.at[core], rel_sem.at[0]).wait()
    finish.wait_send()

    @pl.loop(1, 8)
    def _(d):
        sums(d).wait_send()
        back(d).wait_send()

    out_rows = pl.ds(0, 28 * 8)
    pltpu.make_async_copy(part.at[out_rows], part.at[out_rows], b_send.at[0]).wait()

    @pl.loop(0, 4)
    def _(r):
        @pl.when(4 * y + r != f)
        def _():
            to_owner(y, r, b_own.at[r]).wait_send()


def settle(*refs):
    sources, targets, sem = refs[:4], refs[4:8], refs[8]
    copies = [pltpu.make_async_copy(a, b, sem.at[n]) for n, (a, b) in enumerate(zip(sources, targets))]
    for copy in copies:
        copy.start()
    for copy in copies:
        copy.wait()


def shards(delta, error, param, velocity, piece_ids, piece_counts):
    table = cosine_table(SIDE)
    high, low = halves(table)
    rows_fwd = jnp.asarray(np.concatenate([high, high, low], axis=1))
    rows_inv = jnp.asarray(np.concatenate([high.T, high.T, low.T], axis=1))
    high, low = halves(np.kron(np.eye(2), table.T))
    cols_fwd = jnp.asarray(np.concatenate([high, high, low], axis=0))
    rows, width = param.shape
    any_space = pl.BlockSpec(memory_space=pl.ANY)
    dma = pltpu.SemaphoreType.DMA
    step = width // 4
    results = pl.pallas_call(
        kernel,
        out_shape=(
            pltpu.VMEM(error.shape, F32),
            pltpu.VMEM(param.shape, BF16),
            pltpu.VMEM(param.shape, BF16),
            pltpu.VMEM((1, 32, 16, WIDE), F32),
        ),
        in_specs=[any_space] * 9,
        out_specs=(pl.BlockSpec(memory_space=pltpu.VMEM),) * 4,
        scratch_shapes=[
            pltpu.SMEM((16, 32), jnp.int32),
            pltpu.SMEM((1, 32), jnp.int32),
            pltpu.VMEM((16, 32), jnp.int32),
            pltpu.VMEM((1, 32), jnp.int32),
            pltpu.VMEM((64, 192), BF16),
            pltpu.VMEM((64, 192), BF16),
            pltpu.VMEM((384, 128), BF16),
            pltpu.VMEM((rows, width), BF16),
            pltpu.VMEM((rows, width), F32),
            pltpu.VMEM((rows, width), BF16),
            pltpu.VMEM((rows, width), BF16),
            pltpu.VMEM((2048, WIDE), F32),
            pltpu.VMEM((192, step), BF16),
            pltpu.VMEM((2048, 512), BF16),
            pltpu.VMEM((2048, 512), BF16),
            pltpu.VMEM((64, 128), F32),
            pltpu.VMEM((32, 512), F32),
            pltpu.VMEM((256, WIDE), F32),
            pltpu.VMEM((256, WIDE), F32),
            pltpu.VMEM((256, WIDE), F32),
            pltpu.VMEM((256, WIDE), F32),
            pltpu.VMEM((8, 32, WIDE), F32),
            pltpu.VMEM((2, 256, WIDE), F32),
            pltpu.VMEM((32, WIDE), F32),
            dma((20,)),
            dma((8,)),
            dma((8,)),
            dma((8,)),
            dma((8,)),
            dma((8,)),
            dma((8,)),
            dma((8,)),
            dma((2,)),
            dma((1,)),
            dma((4,)),
            dma((1,)),
            dma((2,)),
            pltpu.SemaphoreType.REGULAR,
            pltpu.SemaphoreType.REGULAR,
        ],
        compiler_params=pltpu.CompilerParams(
            collective_id=0, has_side_effects=True, vmem_limit_bytes=56 << 20),
        name="sync",
    )(delta, error, param, velocity, piece_ids[0].T, piece_counts, rows_fwd, rows_inv, cols_fwd)
    results = [pltpu.with_memory_space_constraint(a, pltpu.VMEM) for a in results]
    return pl.pallas_call(
        settle,
        out_shape=tuple(pltpu.HBM(a.shape, a.dtype) for a in results),
        in_specs=[pl.BlockSpec(memory_space=pltpu.VMEM)] * 4,
        out_specs=(pl.BlockSpec(memory_space=pltpu.HBM),) * 4,
        scratch_shapes=[dma((4,))],
        name="settle",
    )(*results)


def solution(mesh):
    in_specs = (
        P("island", "fsdp", None),
        P("island", "fsdp", None),
        P("fsdp", None),
        P("fsdp", None),
        P("fsdp", None, None),
        P("fsdp", None),
    )
    out_specs = (
        P("island", "fsdp", None),
        P("fsdp", None),
        P("fsdp", None),
        P("fsdp", None, None, None),
    )
    return jax.shard_map(shards, mesh=mesh, in_specs=in_specs, out_specs=out_specs, check_vma=False)
```

```python
import functools
import math

import jax
import jax.numpy as jnp
import ml_dtypes
import numpy as np
from jax import lax
from jax.experimental import pallas as pl
from jax.experimental.pallas import tpu as pltpu
from jax.sharding import PartitionSpec as P

MESH = pl.DeviceIdType.MESH
F32 = jnp.float32
BF16 = jnp.bfloat16

decay_rate = 0.9
outer_rate = 0.7
nesterov = 0.9
eps_value = 1e-06

SIDE = 64
WIDE = 128
PEERS = 7


def far(n):
    return 4 + (1 - 2 * lax.rem(n, 2)) * lax.div(n + 1, 2)


def cosine_table(side):
    freq = np.arange(side, dtype=np.float64)[:, None]
    place = np.arange(side, dtype=np.float64)[None, :]
    scale = np.where(freq == 0, math.sqrt(1.0 / side), math.sqrt(2.0 / side))
    return scale * np.cos(math.pi * (2.0 * place + 1.0) * freq / (2.0 * side))


def halves(table):
    high = table.astype(np.float32).astype(ml_dtypes.bfloat16)
    low = (table - high.astype(np.float64)).astype(ml_dtypes.bfloat16)
    return high, low


def split(values):
    high = values.astype(BF16)
    low = (values - high.astype(F32)).astype(BF16)
    return high, low


def iota(shape, dim):
    return lax.broadcasted_iota(jnp.int32, shape, dim)


def kernel(
    delta, error, param, velocity, ids, counts, rows_fwd, rows_inv, cols_fwd,
    new_error, new_param, new_velocity, compressed,
    ids_s, counts_s, ids_v, counts_v, fwd, inv, cols, d_v, x_v, p_v, v_v, y_v, stack, basis_high, basis_low, mask_v, block_v,
    t_sib, t_own, t_got, part, got, ret, sent,
    in_sem, field_sem, sib_send, sib_recv, rs_send, rs_recv, ag_send, ag_recv, rel_sem, b_send, b_own, b_recv, fin_sem,
    ready_x, ready_y,
):
    i = lax.axis_index("island")
    f = lax.axis_index("fsdp")
    y = lax.div(i, 2)
    core = lax.rem(i, 2)
    z = lax.div(f, 4)
    x = lax.rem(f, 4)
    sibling = (2 * y + (1 - core), f)
    width = error.shape[2]
    step = width // 4
    blocks = step // WIDE

    half = compressed.at[0, :, pl.ds(pl.multiple_of(8 * core, 8), 8), :]

    def share(shard):
        return compressed.at[0, shard, pl.ds(pl.multiple_of(8 * core, 8), 8), :]

    def y_peer(d):
        return (2 * lax.rem(y + d, 8) + core, f)

    barrier = pltpu.get_barrier_semaphore()

    def greet(other):
        pl.semaphore_signal(barrier, inc=1, device_id=other, device_id_type=MESH)

    @pl.loop(0, PEERS)
    def _(n):
        greet(y_peer(far(n)))
        greet((i, 4 * lax.rem(z + far(n), 8) + x))

    @pl.loop(1, 4)
    def _(n):
        greet((i, 4 * z + lax.rem(x + n, 4)))

    opposite = (2 * lax.rem(y + 4, 8) + 1 - core, f)
    greet(opposite)
    greet(sibling)

    loads = {}

    def load(name, src, dst):
        copy = pltpu.make_async_copy(src, dst, in_sem.at[len(loads)])
        copy.start()
        loads[name] = copy

    load("ids_s", ids, ids_s)
    load("fwd", rows_fwd, fwd)

    def columns(c):
        return pl.ds(pl.multiple_of(c * step, step), step)

    def field_loads(c):
        at = columns(c)
        return (
            pltpu.make_async_copy(error.at[0, :, at], x_v.at[:, at], field_sem.at[2 * c]),
            pltpu.make_async_copy(delta.at[0, :, at], d_v.at[:, at], field_sem.at[2 * c + 1]),
        )

    @pl.loop(0, 4)
    def _(c):
        for copy in field_loads(c):
            copy.start()

    load("ids_v", ids, ids_v)
    load("counts_v", counts, counts_v)
    load("counts_s", counts, counts_s)
    load("inv", rows_inv, inv)
    load("cols", cols_fwd, cols)

    loads["fwd"].wait()

    @pl.loop(0, 4)
    def _(c):
        at = columns(c)
        for copy in field_loads(c):
            copy.wait()
        momentum = decay_rate * x_v[:, at] + d_v[:, at].astype(F32)
        x_v[:, at] = momentum
        high, low = split(momentum)
        stack[0:64, :] = high
        stack[64:128, :] = low
        stack[128:192, :] = high
        field = jnp.dot(fwd[...], stack[...], preferred_element_type=F32)
        for j in range(blocks):
            at = pl.ds(pl.multiple_of((c * blocks + j) * SIDE, SIDE), SIDE)
            y_v[at, :] = field[:, j * WIDE:(j + 1) * WIDE]

    loads["ids_s"].wait()

    def gather(side, out, site):
        @pl.loop(0, 4)
        def _(r):
            for k in range(8):
                row = ids_s[8 * side + k, 4 * site + r]
                out[pl.ds(site * 32 + r * 8 + k, 1), :] = y_v[pl.ds(row, 1), :]

    def site_of(n):
        return lax.rem(y + lax.select(n == PEERS, 0, far(n)), 8)

    def rows_of(site):
        return pl.ds(pl.multiple_of(site * 32, 32), 32)

    def exchange(n):
        at = rows_of(site_of(n))
        return pltpu.make_async_remote_copy(
            src_ref=t_sib.at[at], dst_ref=t_got.at[at], send_sem=sib_send.at[n], recv_sem=sib_recv.at[n],
            device_id=sibling, device_id_type=MESH)

    @pl.loop(0, 8)
    def _(n):
        gather(1 - core, t_sib, site_of(n))

    @pl.loop(0, 8)
    def _(n):
        gather(core, t_own, site_of(n))

    pl.semaphore_wait(barrier, 2 * PEERS + 5)

    def direct(source, other, slot):
        return pltpu.make_async_remote_copy(
            src_ref=source.at[rows_of(site_of(0))], dst_ref=got.at[slot],
            send_sem=rs_send.at[slot], recv_sem=rs_recv.at[slot], device_id=other, device_id_type=MESH)

    direct(t_own, y_peer(4), 4).start()
    direct(t_sib, opposite, 0).start()

    @pl.loop(1, 8)
    def _(n):
        exchange(n).start()

    @pl.loop(1, 4)
    def _(n):
        pl.semaphore_signal(ready_x, inc=1, device_id=(i, 4 * z + lax.rem(x + n, 4)), device_id_type=MESH)

    def sums(d):
        at = rows_of(lax.rem(y + d, 8))
        return pltpu.make_async_remote_copy(
            src_ref=part.at[at], dst_ref=got.at[d], send_sem=rs_send.at[d], recv_sem=rs_recv.at[d],
            device_id=y_peer(d), device_id_type=MESH)

    @pl.loop(1, PEERS)
    def _(n):
        at = rows_of(site_of(n))
        exchange(n).wait_recv()
        part[at, :] = t_own[at, :] + t_got[at, :]
        sums(far(n)).start()

    exchange(PEERS).wait_recv()
    mine = pl.ds(pl.multiple_of(y * 32, 32), 32)
    part[mine, :] = t_own[mine, :] + t_got[mine, :]
    pl.semaphore_wait(ready_x, 3)

    @pl.loop(1, 8)
    def _(d):
        pl.semaphore_signal(ready_y, inc=1, device_id=y_peer(d), device_id_type=MESH)

    load("param", param, p_v)
    load("velocity", velocity, v_v)

    loads["ids_v"].wait()
    loads["counts_v"].wait()
    loads["inv"].wait()
    listed = jnp.where(iota((16, 32), 0) < counts_v[...], ids_v[...], -1).astype(F32)
    entry = iota((32, 512), 1)
    pick = jnp.where(iota((32, 512), 0) == (entry // 8) % 32, 1.0, 0.0).astype(F32)
    spread = jnp.dot(listed, pick, precision=lax.Precision.HIGHEST, preferred_element_type=F32)
    entry = iota((16, 512), 1)
    spread = jnp.where(iota((16, 512), 0) == 8 * (entry // 256) + entry % 8, spread, 0.0)
    place = jnp.sum(spread, axis=0, keepdims=True).astype(jnp.int32)
    row_hot = jnp.where(iota((64, 512), 0) == (place & 63), 1.0, 0.0).astype(BF16)
    block_hot = jnp.where(iota((32, 512), 0) == (place >> 6), 1.0, 0.0).astype(BF16)
    mask_v[:, 0:32] = lax.dot_general(row_hot, block_hot, (((1,), (1,)), ((), ())), preferred_element_type=F32)
    block_v[...] = block_hot.astype(F32)
    entry_high = jnp.dot(inv[:, 0:64], row_hot, preferred_element_type=F32)
    entry_low = jnp.dot(inv[:, 128:192], row_hot, preferred_element_type=F32)

    @pl.loop(0, 32)
    def _(q):
        at = pl.ds(pl.multiple_of(q * SIDE, SIDE), SIDE)
        here = block_v[pl.ds(q, 1), :]
        basis_high[at, :] = (entry_high * here).astype(BF16)
        basis_low[at, :] = (entry_low * here).astype(BF16)

    def stack_block(j, values):
        at = pl.ds(j * WIDE, WIDE)
        high, low = split(values)
        stack[0:64, at] = high
        stack[64:128, at] = low
        stack[128:192, at] = high

    @pl.loop(0, 4)
    def _(c):
        at = columns(c)
        mask = pltpu.roll(mask_v[...], WIDE - c * blocks, 1)
        for j in range(blocks):
            rows = pl.ds(pl.multiple_of((c * blocks + j) * SIDE, SIDE), SIDE)
            stack_block(j, y_v[rows, :] * mask[:, j:j + 1])
        kept = jnp.dot(inv[...], stack[...], preferred_element_type=F32)
        new_error[0, :, at] = x_v[:, at] - kept

    loads["counts_s"].wait()
    loads["cols"].wait()

    @pl.loop(0, 8)
    def _(d):
        sums(d).wait_recv()

    total = part[mine, :]
    for d in range(8):
        total = total + got[d]
    alive = []
    for r in range(4):
        live = iota((8, WIDE), 0) + 8 * core < counts_s[0, 4 * y + r]
        alive.append(jnp.where(live, total[8 * r:8 * r + 8], 0.0))
    total = jnp.concatenate(alive, axis=0)
    high, low = split(total)
    spectrum = jnp.dot(jnp.concatenate([high, low, high], axis=1), cols[...], preferred_element_type=F32)
    scale = 1.0 / jnp.sqrt(jnp.mean(total * total, axis=1, keepdims=True) + eps_value)
    sent[...] = spectrum * scale
    ret[core, mine, :] = total * scale
    pl.semaphore_wait(ready_y, 7)

    def to_owner(site, r, sem):
        return pltpu.make_async_remote_copy(
            src_ref=sent.at[pl.ds(pl.multiple_of(8 * r, 8), 8)], dst_ref=share(f), send_sem=sem, recv_sem=b_recv.at[0],
            device_id=(2 * site + core, 4 * y + r), device_id_type=MESH)

    def back(d):
        return pltpu.make_async_remote_copy(
            src_ref=ret.at[core, mine], dst_ref=ret.at[core, mine], send_sem=ag_send.at[d], recv_sem=ag_recv.at[d],
            device_id=y_peer(d), device_id_type=MESH)

    apart = lax.rem(z - y + 8, 8)
    close = jnp.logical_or(apart <= 0, apart >= 8)

    @pl.when(close)
    def _():
        @pl.loop(0, PEERS)
        def _(n):
            back(far(n)).start()

    @pl.loop(0, 4)
    def _(r):
        for n in range(PEERS):
            to_owner(lax.rem(y + (4, 3, 5, 2, 6, 1, 7)[n], 8), r, b_send.at[0]).start()

    @pl.loop(0, 4)
    def _(r):
        @pl.when(4 * y + r == f)
        def _():
            at = pl.ds(pl.multiple_of(8 * r, 8), 8)
            pltpu.make_async_copy(sent.at[at], share(f), b_recv.at[0]).start()

        @pl.when(4 * y + r != f)
        def _():
            to_owner(y, r, b_own.at[r]).start()

    @pl.when(jnp.logical_not(close))
    def _():
        @pl.loop(0, PEERS)
        def _(n):
            back(far(n)).start()


    def relay(d):
        at = pl.ds(pl.multiple_of(lax.rem(y + 8 - d, 8) * 32, 32), 32)
        return pltpu.make_async_remote_copy(
            src_ref=ret.at[core, at], dst_ref=ret.at[core, at], send_sem=rel_sem.at[0], recv_sem=rel_sem.at[1],
            device_id=sibling, device_id_type=MESH)

    relay(0).start()

    @pl.loop(0, PEERS)
    def _(n):
        d = far(PEERS - 1 - n)
        back(d).wait_recv()
        relay(d).start()

    def spread(side, first):
        high, low = split(ret[side])
        both = jnp.concatenate([high, low], axis=1)
        entries = pl.ds(pl.multiple_of(side * 256, 256), 256)

        @pl.loop(0, 4)
        def _(c):
            rows = pl.ds(pl.multiple_of(c * blocks * SIDE, blocks * SIDE), blocks * SIDE)
            fields = jnp.dot(basis_high[rows, entries], both, preferred_element_type=F32)
            field = fields[:, :WIDE] + fields[:, WIDE:]
            field = field + jnp.dot(basis_low[rows, entries], high, preferred_element_type=F32)
            if first:
                y_v[rows, :] = field
            else:
                field = y_v[rows, :] + field
                for j in range(blocks):
                    at = pl.ds(pl.multiple_of((c * blocks + j) * WIDE, WIDE), WIDE)
                    update = field[j * SIDE:(j + 1) * SIDE]
                    moved = nesterov * v_v[:, at].astype(F32) + update
                    step_back = outer_rate * (update + nesterov * moved)
                    new_param[:, at] = (p_v[:, at].astype(F32) - step_back).astype(BF16)
                    new_velocity[:, at] = moved.astype(BF16)

    spread(core, True)

    pltpu.make_async_copy(half, half, b_recv.at[0]).wait()
    finish = pltpu.make_async_remote_copy(
        src_ref=half, dst_ref=half, send_sem=fin_sem.at[0], recv_sem=fin_sem.at[1],
        device_id=sibling, device_id_type=MESH)
    finish.start()
    loads["param"].wait()
    loads["velocity"].wait()
    pltpu.make_async_copy(ret.at[core], ret.at[core], rel_sem.at[1]).wait()
    spread(1 - core, False)
    finish.wait_recv()


    @pl.loop(1, 8)
    def _(n):
        exchange(n).wait_send()

    sums(0).wait_send()
    pltpu.make_async_copy(ret.at[core], ret.at[core], rel_sem.at[0]).wait()
    finish.wait_send()

    @pl.loop(1, 8)
    def _(d):
        sums(d).wait_send()
        back(d).wait_send()

    out_rows = pl.ds(0, 28 * 8)
    pltpu.make_async_copy(part.at[out_rows], part.at[out_rows], b_send.at[0]).wait()

    @pl.loop(0, 4)
    def _(r):
        @pl.when(4 * y + r != f)
        def _():
            to_owner(y, r, b_own.at[r]).wait_send()


def settle(*refs):
    sources, targets, sem = refs[:4], refs[4:8], refs[8]
    copies = [pltpu.make_async_copy(a, b, sem.at[n]) for n, (a, b) in enumerate(zip(sources, targets))]
    for copy in copies:
        copy.start()
    for copy in copies:
        copy.wait()


def shards(delta, error, param, velocity, piece_ids, piece_counts):
    table = cosine_table(SIDE)
    high, low = halves(table)
    rows_fwd = jnp.asarray(np.concatenate([high, high, low], axis=1))
    rows_inv = jnp.asarray(np.concatenate([high.T, high.T, low.T], axis=1))
    high, low = halves(np.kron(np.eye(2), table.T))
    cols_fwd = jnp.asarray(np.concatenate([high, high, low], axis=0))
    rows, width = param.shape
    any_space = pl.BlockSpec(memory_space=pl.ANY)
    dma = pltpu.SemaphoreType.DMA
    step = width // 4
    results = pl.pallas_call(
        kernel,
        out_shape=(
            pltpu.VMEM(error.shape, F32),
            pltpu.VMEM(param.shape, BF16),
            pltpu.VMEM(param.shape, BF16),
            pltpu.VMEM((1, 32, 16, WIDE), F32),
        ),
        in_specs=[any_space] * 9,
        out_specs=(pl.BlockSpec(memory_space=pltpu.VMEM),) * 4,
        scratch_shapes=[
            pltpu.SMEM((16, 32), jnp.int32),
            pltpu.SMEM((1, 32), jnp.int32),
            pltpu.VMEM((16, 32), jnp.int32),
            pltpu.VMEM((1, 32), jnp.int32),
            pltpu.VMEM((64, 192), BF16),
            pltpu.VMEM((64, 192), BF16),
            pltpu.VMEM((384, 128), BF16),
            pltpu.VMEM((rows, width), BF16),
            pltpu.VMEM((rows, width), F32),
            pltpu.VMEM((rows, width), BF16),
            pltpu.VMEM((rows, width), BF16),
            pltpu.VMEM((2048, WIDE), F32),
            pltpu.VMEM((192, step), BF16),
            pltpu.VMEM((2048, 512), BF16),
            pltpu.VMEM((2048, 512), BF16),
            pltpu.VMEM((64, 128), F32),
            pltpu.VMEM((32, 512), F32),
            pltpu.VMEM((256, WIDE), F32),
            pltpu.VMEM((256, WIDE), F32),
            pltpu.VMEM((256, WIDE), F32),
            pltpu.VMEM((256, WIDE), F32),
            pltpu.VMEM((8, 32, WIDE), F32),
            pltpu.VMEM((2, 256, WIDE), F32),
            pltpu.VMEM((32, WIDE), F32),
            dma((20,)),
            dma((8,)),
            dma((8,)),
            dma((8,)),
            dma((8,)),
            dma((8,)),
            dma((8,)),
            dma((8,)),
            dma((2,)),
            dma((1,)),
            dma((4,)),
            dma((1,)),
            dma((2,)),
            pltpu.SemaphoreType.REGULAR,
            pltpu.SemaphoreType.REGULAR,
        ],
        compiler_params=pltpu.CompilerParams(
            collective_id=0, has_side_effects=True, vmem_limit_bytes=56 << 20),
        name="sync",
    )(delta, error, param, velocity, piece_ids[0].T, piece_counts, rows_fwd, rows_inv, cols_fwd)
    results = [pltpu.with_memory_space_constraint(a, pltpu.VMEM) for a in results]
    return pl.pallas_call(
        settle,
        out_shape=tuple(pltpu.HBM(a.shape, a.dtype) for a in results),
        in_specs=[pl.BlockSpec(memory_space=pltpu.VMEM)] * 4,
        out_specs=(pl.BlockSpec(memory_space=pltpu.HBM),) * 4,
        scratch_shapes=[dma((4,))],
        name="settle",
    )(*results)


def solution(mesh):
    in_specs = (
        P("island", "fsdp", None),
        P("island", "fsdp", None),
        P("fsdp", None),
        P("fsdp", None),
        P("fsdp", None, None),
        P("fsdp", None),
    )
    out_specs = (
        P("island", "fsdp", None),
        P("fsdp", None),
        P("fsdp", None),
        P("fsdp", None, None, None),
    )
    return jax.shard_map(shards, mesh=mesh, in_specs=in_specs, out_specs=out_specs, check_vma=False)
```
